128 devices in a mesh: frame: 4 (over z_lo, core), tile: 32 (over y, x, z_hi).
Axes of the slice: x: 4, y: 4, z: 4 (z_hi: 2, z_lo: 2; z = z_hi * 2 + z_lo), core: 2. Of those that a mesh axis runs over, the one named last changes fastest.
Arguments:
- frames: bfloat16 [4, 64, 256, 2048], P('frame', None, 'tile'), may hold values from -6 to 6
- predict_w: bfloat16 [2, 4, 3, 3, 64, 64], replicated, may hold values from -0.25 to 0.25
- predict_b: float32 [2, 4, 64], replicated, may hold values from -2 to 2
- update_w: bfloat16 [2, 4, 3, 3, 64, 64], replicated, may hold values from -0.25 to 0.25
- update_b: float32 [2, 4, 64], replicated, may hold values from -2 to 2
Outputs:
- coefficients: bfloat16 [4, 64, 256, 2048], P('frame', None, 'tile')
The draws below stay inside these ranges and needn't reach their ends.
All inputs are finite; a program needn't handle non-finite values.
Results may differ from the reference program's by a relative error of at most 0.009.
Values may be sent and summed in bfloat16 or wider, within the bound.
No kernel may reach another device: no remote copies, remote signals or barrier semaphores. Data moves between devices by JAX's collectives and lax.ppermute only.
A program may use at most 128 MiB of HBM per device.

```python
import jax
import jax.numpy as jnp
from jax import lax

C = 64
W = 2048
LAYERS = 4
FRAMES = 4
H = 256


def shard_levels(own_key, dims, shards, low, top_value):
    loudness, own = 1.0, jax.random.fold_in(own_key, 6)
    for dim, blocks in shards:
        heights = jnp.exp(jax.random.uniform(jax.random.fold_in(own, dim), (blocks,), jnp.float32, low / len(shards), top_value / len(shards)))
        loudness = loudness * jnp.repeat(heights, dims[dim] // blocks).reshape([-1 if axis == dim else 1 for axis in range(len(dims))])
    return loudness


def normal_values(stream_key, dims, width, reach, cuts=(), held_as=jnp.bfloat16):
    array = jax.random.normal(stream_key, dims, jnp.float32) * width
    if len(cuts) > 0:
        array = shard_levels(stream_key, dims, cuts, -0.22, 0.18) * array
    return jnp.clip(array, min=-reach, max=reach).astype(held_as)


def setup_inputs(seed: int = 0) -> dict:
    keys = jax.random.split(jax.random.key(seed), 6)
    return {
        "frames": normal_values(keys[0], (FRAMES, C, H, W), 1.0, 6.0, ((0, 4), (2, 32))),
        "predict_w": normal_values(keys[1], (2, LAYERS, 3, 3, C, C), (9 * C) ** -0.5, 0.25),
        "predict_b": normal_values(keys[2], (2, LAYERS, C), 0.3, 2.0, (), jnp.float32),
        "update_w": normal_values(keys[3], (2, LAYERS, 3, 3, C, C), (9 * C) ** -0.5, 0.25),
        "update_b": normal_values(keys[4], (2, LAYERS, C), 0.3, 2.0, (), jnp.float32),
    }


def conv_layer(field, kernel, bias_row):
    weights = jnp.transpose(kernel.astype(jnp.float32), (2, 3, 0, 1))
    result = lax.conv_general_dilated(field, weights, (1, 1), ((1, 1), (1, 1)), dimension_numbers=("NCHW", "OIHW", "NCHW"), precision=lax.Precision.HIGHEST)
    return result + bias_row[None, :, None, None]


def network(field, kernels, biases):
    hidden = field.astype(jnp.float32)
    for layer_index in range(LAYERS):
        result = conv_layer(hidden, kernels[layer_index], biases[layer_index])
        if layer_index < LAYERS - 1:
            rounded = lax.optimization_barrier(jnp.maximum(result, 0.0).astype(jnp.bfloat16))
            hidden = rounded.astype(jnp.float32)
    return result


def reference(frames, predict_w, predict_b, update_w, update_b):
    even_frames = frames[0::2]
    odd_frames = frames[1::2]
    high_one = (odd_frames.astype(jnp.float32) - network(even_frames, predict_w[0], predict_b[0])).astype(jnp.bfloat16)
    low_one = (even_frames.astype(jnp.float32) + network(high_one, update_w[0], update_b[0])).astype(jnp.bfloat16)
    low_even = low_one[0::2]
    low_odd = low_one[1::2]
    high_two = (low_odd.astype(jnp.float32) - network(low_even, predict_w[1], predict_b[1])).astype(jnp.bfloat16)
    low_two = (low_even.astype(jnp.float32) + network(high_two, update_w[1], update_b[1])).astype(jnp.bfloat16)
    stacked = jnp.stack([low_two, high_one[0::2], high_two, high_one[1::2]], axis=1)
    return stacked.reshape(frames.shape)
```

```python
import functools

import jax
import jax.numpy as jnp
from jax import lax
from jax.experimental import pallas as pl
from jax.experimental.pallas import tpu as pltpu
from jax.sharding import PartitionSpec as P

LAYERS = 4
C = 64
ROWS = 16
LANES = 384
OWN = 256
EDGE = 64
BF16 = jnp.bfloat16
F32 = jnp.float32
VMEM_LIMIT = 48 * 1024 * 1024


def call(kernel, out_shapes, scratch, flops, name, *args):
    nbytes = sum(a.size * a.dtype.itemsize for a in args) + sum(
        s.size * s.dtype.itemsize for s in out_shapes
    )
    return pl.pallas_call(
        kernel,
        out_shape=out_shapes,
        in_specs=[pl.BlockSpec(memory_space=pltpu.SMEM)]
        + [pl.BlockSpec(memory_space=pltpu.VMEM)] * (len(args) - 1),
        out_specs=[pl.BlockSpec(memory_space=pltpu.VMEM)] * len(out_shapes),
        scratch_shapes=scratch,
        compiler_params=pltpu.CompilerParams(vmem_limit_bytes=VMEM_LIMIT),
        cost_estimate=pl.CostEstimate(flops=flops, bytes_accessed=nbytes, transcendentals=0),
        name=name,
    )(*args)


def field(*dims):
    return jax.ShapeDtypeStruct(dims, BF16)


def split_kernel(which, place, x_ref, out_ref, spread):
    core = place[1]
    source = lax.broadcasted_iota(jnp.int32, (512, LANES), 0)
    column = lax.broadcasted_iota(jnp.int32, (512, LANES), 1)
    pick = jnp.where(source == 3 * (column % 128) + column // 128 + 128 - EDGE, 1.0, 0.0)
    pick = pick.astype(BF16)

    def windows(group):
        for slot in range(4):
            start = 256 * (4 * group + slot) - 128
            low, high = max(start, 0), min(start + 512, 2048)
            window = jnp.dot(
                x_ref[:, low:high], pick[low - start : high - start], preferred_element_type=F32
            )
            for v in range(3):
                spread[v] = window[:, 128 * v : 128 * (v + 1)]
            for row in range(8):
                out_ref[slot, row] = jnp.concatenate(
                    [spread[v, pl.ds(row, C, stride=8), :] for v in range(3)], axis=1
                ).astype(BF16)

    for group in range(2):
        pl.when((core ^ which) == group)(functools.partial(windows, group))


def own_columns(value):
    source = lax.broadcasted_iota(jnp.int32, (LANES, OWN), 0)
    column = lax.broadcasted_iota(jnp.int32, (LANES, OWN), 1)
    pick = jnp.where(3 * (source % 128) + source // 128 == column + EDGE, 1.0, 0.0).astype(BF16)
    rows = value.shape[0]
    flat = jnp.dot(value.reshape(rows * C, LANES), pick, preferred_element_type=F32)
    return flat.astype(BF16).reshape(rows, C, OWN)


def join_kernel(place, *refs):
    pieces, out_ref, spread = refs[:16], refs[16], refs[17]
    chip, core = place[0], place[1]

    def joined(group):
        for side in range(2):
            for other in range(4):
                piece = pieces[8 * group + 4 * side + other]
                for row in range(8):
                    values = piece[row].astype(F32)
                    for v in range(2):
                        spread[v, pl.ds(row, C, stride=8), :] = values[:, 128 * v : 128 * (v + 1)]
                window = 4 * (group ^ side) + (chip ^ other)
                for v in range(2):
                    column = pl.multiple_of(window * OWN + 128 * v, 128)
                    out_ref[:, pl.ds(column, 128)] = spread[v].astype(BF16)

    for group in range(2):
        pl.when(core == group)(functools.partial(joined, group))


def edges(place):
    lane = lax.broadcasted_iota(jnp.int32, (1, 128), 1)
    window = 4 * place[1] + place[0]
    left = jnp.where((lane == 21) & (window == 0), 0.0, 1.0)
    right = jnp.where((lane == 106) & (window == 7), 0.0, 1.0)
    top = jnp.where(place[2] == 0, 0.0, 1.0)
    bottom = jnp.where(place[2] == 15, 0.0, 1.0)
    return left, right, top, bottom


def conv(source, count, weights, bias, left, right, store):
    pairs = count // 2
    stack = jnp.concatenate(
        [source[2 * j : 2 * j + 4].reshape(4 * C, LANES) for j in range(pairs)], axis=1
    )
    product = jnp.dot(weights, stack, preferred_element_type=F32)
    for j in range(pairs):
        part = [
            [
                product[2 * C * s : 2 * C * (s + 1), LANES * j + 128 * v : LANES * j + 128 * (v + 1)]
                for v in range(3)
            ]
            for s in range(3)
        ]
        blocks = [
            pltpu.roll(part[0][2], 1, 1) + part[1][0] + part[2][1] + bias,
            part[0][0] * left + part[1][1] + part[2][2] * right + bias,
            part[0][1] + part[1][2] + pltpu.roll(part[2][0], 127, 1) + bias,
        ]
        total = jnp.concatenate(blocks, axis=1)
        store(2 * j, total[:C])
        store(2 * j + 1, total[C:])


def network(source, spare, halo, weights, biases, edge, finish):
    left, right, top, bottom = edge
    count = source.shape[0]
    for layer in range(LAYERS):
        count -= 2
        target = spare[layer % 2]

        def keep(row, value, layer=layer, target=target):
            value = jnp.maximum(value, 0.0)
            ahead = row - (halo - layer - 1)
            if ahead == -1:
                value = value * top
            if ahead == ROWS:
                value = value * bottom
            target[row] = value.astype(BF16)

        store = keep if layer < LAYERS - 1 else finish
        conv(source, count, weights[layer], biases[layer], left, right, store)
        source = target


def place_halo(field_ref, first, second, depth, ring_is_odd):
    low, high = 0, depth + ROWS
    field_ref[pl.ds(jnp.where(ring_is_odd, low, high), depth)] = first
    field_ref[pl.ds(jnp.where(ring_is_odd, high, low), depth)] = second


def place_pieces(field_ref, pieces, pair, chip, offset):
    for other in range(4):
        slot = chip ^ other

        @pl.when((slot & 1) == pair)
        def _(other=other, slot=slot):
            field_ref[pl.ds(offset + 8 * (slot // 2), 8)] = pieces[other][...]


def strips(result, first_ref, second_ref, depth, ring_is_odd):
    first_ref[...] = result[pl.ds(jnp.where(ring_is_odd, 0, ROWS - depth), depth)]
    second_ref[...] = result[pl.ds(jnp.where(ring_is_odd, ROWS - depth, 0), depth)]


def predict_kernel(pair, place, *refs):
    evens, odds = refs[0:4], refs[4:8]
    halo_a, halo_b, weights, biases = refs[8:12]
    refs = refs[12:]
    if pair == 1:
        own_zero, refs = refs[0], refs[1:]
    high, strip_a, strip_b = refs[:3]
    outs, (source, spare_a, spare_b, target) = refs[3:-4], refs[-4:]
    chip, odd_ring = place[0], place[2] % 2 == 1
    place_pieces(source, evens, pair, chip, LAYERS)
    place_halo(source, halo_a[pair], halo_b[pair], LAYERS, odd_ring)
    place_pieces(target, odds, pair, chip, 0)

    def finish(row, value):
        high[row] = (target[row].astype(F32) - value).astype(BF16)

    network(source, (spare_a, spare_b), LAYERS, weights, biases, edges(place), finish)
    strips(high, strip_a, strip_b, LAYERS, odd_ring)
    own = own_columns(high[...])
    if pair == 0:
        outs[0][...] = own
    else:
        for other in range(4):
            slot = chip ^ other
            for half in range(2):
                for which in range(2):

                    @pl.when(slot == 2 * half + which)
                    def _(other=other, half=half, which=which):
                        rows = slice(8 * half, 8 * half + 8)
                        outs[other][...] = own_zero[rows] if which == 0 else own[rows]


def update_kernel(pair, depth, place, *refs):
    high, halo_a, halo_b = refs[0:3]
    evens = refs[3:7]
    weights, biases = refs[7:9]
    low, strip_a, strip_b, source, spare_a, spare_b, target = refs[9:]
    odd_ring = place[2] % 2 == 1
    source[LAYERS : LAYERS + ROWS] = high[...]
    place_halo(source, halo_a[...], halo_b[...], LAYERS, odd_ring)
    place_pieces(target, evens, pair, place[0], 0)

    def finish(row, value):
        low[row] = (target[row].astype(F32) + value).astype(BF16)

    network(source, (spare_a, spare_b), LAYERS, weights, biases, edges(place), finish)
    strips(low, strip_a, strip_b, depth, odd_ring)


def second_kernel(place, *refs):
    low_even, even_a, even_b, low_odd, odd_a, odd_b = refs[0:6]
    predict_w, predict_b, update_w, update_b = refs[6:10]
    outs = refs[10:14]
    source, target, spare_a, spare_b, high, low, slots = refs[14:]
    chip, odd_ring = place[0], place[2] % 2 == 1
    edge = edges(place)
    top, bottom = edge[2:]
    source[2 * LAYERS : 2 * LAYERS + ROWS] = low_even[...]
    place_halo(source, even_a[...], even_b[...], 2 * LAYERS, odd_ring)
    target[LAYERS : LAYERS + ROWS] = low_odd[...]
    place_halo(target, odd_a[...], odd_b[...], LAYERS, odd_ring)

    def finish_high(row, value):
        value = target[row].astype(F32) - value
        if row == LAYERS - 1:
            value = value * top
        if row == LAYERS + ROWS:
            value = value * bottom
        high[row] = value.astype(BF16)

    network(source, (spare_a, spare_b), 2 * LAYERS, predict_w, predict_b, edge, finish_high)

    def finish_low(row, value):
        low[row] = (low_even[row].astype(F32) + value).astype(BF16)

    network(high, (spare_a, spare_b), LAYERS, update_w, update_b, edge, finish_low)
    own_low = own_columns(low[...])
    own_high = own_columns(high[LAYERS : LAYERS + ROWS])
    for half in range(2):
        slots[2 * half] = own_low[8 * half : 8 * half + 8]
        slots[2 * half + 1] = own_high[8 * half : 8 * half + 8]
    for other in range(4):
        outs[other][...] = slots[chip ^ other]


def toeplitz(kernels):
    by_column = jnp.transpose(kernels, (0, 1, 3, 4, 2, 5)).reshape(2, LAYERS, 3, C, 3 * C)
    pad = ((0, 0),) * 4
    upper = jnp.pad(by_column, (*pad, (0, C)))
    lower = jnp.pad(by_column, (*pad, (C, 0)))
    return jnp.stack([upper, lower], axis=3).reshape(2, LAYERS, 6 * C, 4 * C)


def spread_bias(biases):
    return jnp.broadcast_to(jnp.tile(biases, (1, 1, 2))[..., None], (2, LAYERS, 2 * C, 128))


def to_core(x):
    return lax.ppermute(x, "frame", [(i, i ^ 1) for i in range(4)])


def to_chip(x, other):
    if other == 0:
        return x
    if other == 1:
        return lax.ppermute(x, "frame", [(i, i ^ 2) for i in range(4)])
    tiles = lax.axis_size("tile")
    if other == 2:
        return lax.ppermute(x, "tile", [(i, i ^ 1) for i in range(tiles)])
    return lax.ppermute(
        x,
        ("frame", "tile"),
        [(f * tiles + t, (f ^ 2) * tiles + (t ^ 1)) for f in range(4) for t in range(tiles)],
    )


def with_rings(first, second):
    tiles = lax.axis_size("tile")
    one = [(t, t ^ 2) for t in range(tiles)]
    two = []
    for t in range(tiles):
        target = t + 2 if (t // 2) % 2 == 1 else t - 2
        if 0 <= target < tiles:
            two.append((t, target))
    return lax.ppermute(first, "tile", one), lax.ppermute(second, "tile", two)


def local(frames, predict_w, predict_b, update_w, update_b):
    position, tile = lax.axis_index("frame"), lax.axis_index("tile")
    core = position % 2
    chip = 2 * (tile % 2) + position // 2
    ring = tile // 2
    place = jnp.stack([chip, core, ring]).astype(jnp.int32)
    odd_ring = ring % 2 == 1
    x = frames[0].reshape(8 * C, 2048)

    layer_flops = 2 * 6 * C * 4 * C * LANES // 2

    def split(which):
        (out,) = call(
            functools.partial(split_kernel, which),
            [field(4, 8, C, LANES)],
            [pltpu.VMEM((3, 8 * C, 128), F32)],
            2 * 4 * 512 * 512 * LANES,
            f"split_{which}",
            place,
            x,
        )
        return out

    passed = to_core(split(1))
    kept = split(0)
    is_even = core == 0
    evens, odds = [], []
    for other in range(4):
        mine = lax.dynamic_index_in_dim(kept, chip ^ other, 0, False)
        theirs = lax.dynamic_index_in_dim(passed, chip ^ other, 0, False)
        evens.append(to_chip(jnp.where(is_even, mine, theirs), other))
        odds.append(jnp.where(is_even, theirs, mine))
    held = lax.optimization_barrier((*odds, *evens))
    odds = [to_chip(x, other) for other, x in enumerate(held[:4])]
    evens = list(held[4:])

    tops = jnp.stack([lax.select_n(p ^ chip, *[e[:LAYERS] for e in evens]) for p in range(2)])
    bottoms = jnp.stack(
        [lax.select_n((2 + p) ^ chip, *[e[8 - LAYERS :] for e in evens]) for p in range(2)]
    )
    halo = with_rings(
        jnp.where(odd_ring, tops, bottoms), jnp.where(odd_ring, bottoms, tops)
    )

    pw, uw = toeplitz(predict_w), toeplitz(update_w)
    pb, ub = spread_bias(predict_b), spread_bias(update_b)

    def scratch(rows):
        return [pltpu.VMEM((count, C, LANES), BF16) for count in rows]

    net_flops = 76 * layer_flops
    strip = field(LAYERS, C, LANES)
    whole = field(ROWS, C, LANES)
    owned = field(8, C, OWN)
    high, halo_high, own_zero = [], [], None
    for pair in range(2):
        outs = [field(ROWS, C, OWN)] if pair == 0 else [owned] * 4
        extra = [] if pair == 0 else [own_zero]
        result, strip_a, strip_b, *owns = call(
            functools.partial(predict_kernel, pair),
            [whole, strip, strip, *outs],
            scratch([24, 22, 20, ROWS]),
            net_flops,
            f"predict_{pair}",
            place,
            *evens,
            *odds,
            *halo,
            pw[0],
            pb[0],
            *extra,
        )
        own_zero = owns[0]
        high.append(result)
        halo_high.append(with_rings(strip_a, strip_b))
    ones = [to_chip(x, other) for other, x in enumerate(owns)]
    ones_other = [to_core(x) for x in ones]

    low, halo_low = [], []
    for pair in range(2):
        depth = 2 * LAYERS if pair == 0 else LAYERS
        result, strip_a, strip_b = call(
            functools.partial(update_kernel, pair, depth),
            [whole, field(depth, C, LANES), field(depth, C, LANES)],
            scratch([24, 22, 20, ROWS]),
            net_flops,
            f"update_{pair}",
            place,
            high[pair],
            *halo_high[pair],
            *evens,
            uw[0],
            ub[0],
        )
        low.append(result)
        halo_low.append(with_rings(strip_a, strip_b))

    owns = call(
        second_kernel,
        [owned] * 4,
        scratch([32, 24, 30, 28, 24, ROWS]) + [pltpu.VMEM((4, 8, C, OWN), BF16)],
        184 * layer_flops,
        "second_level",
        place,
        low[0],
        *halo_low[0],
        low[1],
        *halo_low[1],
        pw[1],
        pb[1],
        uw[1],
        ub[1],
    )
    twos = [to_chip(x, other) for other, x in enumerate(owns)]
    twos_other = [to_core(x) for x in twos]
    (out,) = call(
        join_kernel,
        [field(8 * C, 2048)],
        [pltpu.VMEM((2, 8 * C, 128), F32)],
        0,
        "join",
        place,
        *twos,
        *twos_other,
        *ones,
        *ones_other,
    )
    return out.reshape(1, C, 8, 2048)


def solution(mesh):
    in_specs = (P("frame", None, "tile", None), P(), P(), P(), P())
    out_specs = P("frame", None, "tile", None)
    return jax.shard_map(local, mesh=mesh, in_specs=in_specs, out_specs=out_specs, check_vma=False)
```

```python
import functools

import jax
import jax.numpy as jnp
from jax import lax
from jax.experimental import pallas as pl
from jax.experimental.pallas import tpu as pltpu
from jax.sharding import PartitionSpec as P

LAYERS = 4
C = 64
ROWS = 16
LANES = 384
OWN = 256
EDGE = 64
BF16 = jnp.bfloat16
F32 = jnp.float32
VMEM_LIMIT = 24 * 1024 * 1024
GROUP = 4


def call(kernel, out_shapes, scratch, flops, name, *args):
    nbytes = sum(a.size * a.dtype.itemsize for a in args) + sum(
        s.size * s.dtype.itemsize for s in out_shapes
    )
    return pl.pallas_call(
        kernel,
        out_shape=out_shapes,
        in_specs=[pl.BlockSpec(memory_space=pltpu.SMEM)]
        + [pl.BlockSpec(memory_space=pltpu.VMEM)] * (len(args) - 1),
        out_specs=[pl.BlockSpec(memory_space=pltpu.VMEM)] * len(out_shapes),
        scratch_shapes=scratch,
        compiler_params=pltpu.CompilerParams(vmem_limit_bytes=VMEM_LIMIT),
        cost_estimate=pl.CostEstimate(flops=flops, bytes_accessed=nbytes, transcendentals=0),
        name=name,
    )(*args)


def field(*dims):
    return jax.ShapeDtypeStruct(dims, BF16)


def rolled(value, amount):
    return jnp.concatenate(
        [pltpu.roll(value[:, 128 * v : 128 * (v + 1)], amount % 128, 1) for v in range(3)], axis=1
    )


def lane_in_block():
    return lax.broadcasted_iota(jnp.int32, (C, LANES), 1) % 128


def packed(rows):
    lane = lane_in_block()
    free = (lane < 16) | (lane >= 112)
    return [jnp.where(free, rolled(rows[3], 96 - 32 * j), rows[j]) for j in range(3)]


def unpacked(rows):
    lane = lane_in_block()
    parts = [rolled(rows[j], 32 * j - 96) for j in range(3)]
    fourth = jnp.where(lane < 48, parts[0], jnp.where(lane < 80, parts[1], parts[2]))
    return [*rows, fourth]


def unpack_into(field_ref, start, source, count):
    for group in range(count // 4):
        rows = unpacked([source[3 * group + j] for j in range(3)])
        for j in range(4):
            field_ref[start + 4 * group + j] = rows[j]


def split_kernel(which, place, x_ref, out_ref, spread):
    core = place[1]
    source = lax.broadcasted_iota(jnp.int32, (512, LANES), 0)
    column = lax.broadcasted_iota(jnp.int32, (512, LANES), 1)
    pick = jnp.where(source == 3 * (column % 128) + column // 128 + 128 - EDGE, 1.0, 0.0)
    pick = pick.astype(BF16)

    def windows(group):
        for slot in range(4):
            start = 256 * (4 * group + slot) - 128
            low, high = max(start, 0), min(start + 512, 2048)
            window = jnp.dot(
                x_ref[:, low:high], pick[low - start : high - start], preferred_element_type=F32
            )
            for v in range(3):
                spread[v] = window[:, 128 * v : 128 * (v + 1)]
            for half in range(2):
                rows = packed(
                    [
                        jnp.concatenate(
                            [spread[v, pl.ds(row, C, stride=8), :] for v in range(3)], axis=1
                        ).astype(BF16)
                        for row in range(4 * half, 4 * half + 4)
                    ]
                )
                for j in range(3):
                    out_ref[slot, 3 * half + j] = rows[j]

    for group in range(2):
        pl.when((core ^ which) == group)(functools.partial(windows, group))


def own_columns(value):
    source = lax.broadcasted_iota(jnp.int32, (LANES, OWN), 0)
    column = lax.broadcasted_iota(jnp.int32, (LANES, OWN), 1)
    pick = jnp.where(3 * (source % 128) + source // 128 == column + EDGE, 1.0, 0.0).astype(BF16)
    rows = value.shape[0]
    flat = jnp.dot(value.reshape(rows * C, LANES), pick, preferred_element_type=F32)
    return flat.astype(BF16).reshape(rows, C, OWN)


def join_kernel(place, *refs):
    pieces, out_ref, spread = refs[:16], refs[16], refs[17]
    chip, core = place[0], place[1]

    def joined(group):
        for side in range(2):
            for other in range(4):
                piece = pieces[8 * group + 4 * side + other]
                for row in range(8):
                    values = piece[row].astype(F32)
                    for v in range(2):
                        spread[v, pl.ds(row, C, stride=8), :] = values[:, 128 * v : 128 * (v + 1)]
                window = 4 * (group ^ side) + (chip ^ other)
                for v in range(2):
                    column = pl.multiple_of(window * OWN + 128 * v, 128)
                    out_ref[:, pl.ds(column, 128)] = spread[v].astype(BF16)

    for group in range(2):
        pl.when(core == group)(functools.partial(joined, group))


def edges(place):
    lane = lax.broadcasted_iota(jnp.int32, (1, 128), 1)
    window = 4 * place[1] + place[0]
    left = jnp.where((lane == 21) & (window == 0), 0.0, 1.0)
    right = jnp.where((lane == 106) & (window == 7), 0.0, 1.0)
    top = jnp.where(place[2] == 0, 0.0, 1.0)
    bottom = jnp.where(place[2] == 15, 0.0, 1.0)
    return left, right, top, bottom


def conv(source, count, weights, bias, left, right, store):
    for first in range(0, count // 2, GROUP):
        pairs = range(first, min(first + GROUP, count // 2))
        stack = jnp.concatenate(
            [source[2 * j : 2 * j + 4].reshape(4 * C, LANES) for j in pairs], axis=1
        )
        product = jnp.dot(weights, stack, preferred_element_type=F32)
        for place, j in enumerate(pairs):
            part = [
                [
                    product[
                        2 * C * s : 2 * C * (s + 1),
                        LANES * place + 128 * v : LANES * place + 128 * (v + 1),
                    ]
                    for v in range(3)
                ]
                for s in range(3)
            ]
            blocks = [
                pltpu.roll(part[0][2], 1, 1) + part[1][0] + part[2][1] + bias,
                part[0][0] * left + part[1][1] + part[2][2] * right + bias,
                part[0][1] + part[1][2] + pltpu.roll(part[2][0], 127, 1) + bias,
            ]
            total = jnp.concatenate(blocks, axis=1)
            store(2 * j, total[:C])
            store(2 * j + 1, total[C:])


def hidden_layers(source, targets, halo, weights, biases, edge):
    left, right, top, bottom = edge
    for layer, target in enumerate(targets):
        halo -= 1
        count = source.shape[0] - 2

        def keep(row, value, halo=halo, target=target):
            value = jnp.maximum(value, 0.0)
            if row == halo - 1:
                value = value * top
            if row == halo + ROWS:
                value = value * bottom
            target[row] = value.astype(BF16)

        conv(source, count, weights[layer], biases[layer], left, right, keep)
        source = target
    return source


def lift(third, target, base, high, spares, weights, low, edge):
    predict_w, predict_b, update_w, update_b = weights
    left, right, top, bottom = edge

    def finish_high(row, value):
        value = target[row].astype(F32) - value
        if row == LAYERS - 1:
            value = value * top
        if row == LAYERS + ROWS:
            value = value * bottom
        high[row] = value.astype(BF16)

    conv(third, ROWS + 8, predict_w[3], predict_b[3], left, right, finish_high)

    def finish_low(row, value):
        low[row] = (base[row].astype(F32) + value).astype(BF16)

    source = hidden_layers(high, spares, LAYERS, update_w, update_b, edge)
    conv(source, ROWS, update_w[3], update_b[3], left, right, finish_low)


def place_halo(field_ref, first, second, depth, ring_is_odd):
    low, high = 0, depth + ROWS
    unpack_into(field_ref, jnp.where(ring_is_odd, low, high), first, depth)
    unpack_into(field_ref, jnp.where(ring_is_odd, high, low), second, depth)


def place_pieces(field_ref, pieces, pair, chip, offset):
    for other in range(4):
        slot = chip ^ other

        @pl.when((slot & 1) == pair)
        def _(other=other, slot=slot):
            unpack_into(field_ref, offset + 8 * (slot // 2), pieces[other], 8)


def strips(result, first_ref, second_ref, depth, ring_is_odd):
    for ref, start in (
        (first_ref, jnp.where(ring_is_odd, 0, ROWS - depth)),
        (second_ref, jnp.where(ring_is_odd, ROWS - depth, 0)),
    ):
        for group in range(depth // 4):
            rows = packed([result[start + 4 * group + j] for j in range(4)])
            for j in range(3):
                ref[3 * group + j] = rows[j]


def first_hidden_kernel(place, *refs):
    evens, halo_a, halo_b, weights, biases, out, source, spare_a, spare_b = (refs[:4], *refs[4:])
    chip, odd_ring = place[0], place[2] % 2 == 1
    for pair in range(2):
        entry = (chip & 1) ^ pair
        place_pieces(source, evens, pair, chip, 2 * LAYERS)
        place_halo(source, halo_a.at[entry], halo_b.at[entry], 2 * LAYERS, odd_ring)
        targets = (spare_a, spare_b, out.at[pair])
        hidden_layers(source, targets, 2 * LAYERS, weights, biases, edges(place))


def second_hidden_kernel(place, *refs):
    low_even, halo_a, halo_b, weights, biases, out, source, spare_a, spare_b = refs
    odd_ring = place[2] % 2 == 1
    source[2 * LAYERS : 2 * LAYERS + ROWS] = low_even[...]
    place_halo(source, halo_a, halo_b, 2 * LAYERS, odd_ring)
    targets = (spare_a, spare_b, out)
    hidden_layers(source, targets, 2 * LAYERS, weights, biases, edges(place))


def first_lift_kernel(pair, depth, place, *refs):
    third, evens, odds, halo_a, halo_b = refs[0], refs[1:5], refs[5:9], refs[9], refs[10]
    weights, refs = refs[11:15], refs[15:]
    if pair == 1:
        own_zero, refs = refs[0], refs[1:]
    low, strip_a, strip_b = refs[:3]
    outs, (target, base, high, *spares) = refs[3:-6], refs[-6:]
    chip, odd_ring = place[0], place[2] % 2 == 1
    entry = (chip & 1) ^ pair
    place_pieces(target, odds, pair, chip, LAYERS)
    place_halo(target, halo_a.at[entry], halo_b.at[entry], LAYERS, odd_ring)
    place_pieces(base, evens, pair, chip, 0)
    lift(third.at[pair], target, base, high, spares, weights, low, edges(place))
    strips(low, strip_a, strip_b, depth, odd_ring)
    own = own_columns(high[LAYERS : LAYERS + ROWS])
    if pair == 0:
        outs[0][...] = own
    else:
        for other in range(4):
            slot = chip ^ other
            for half in range(2):
                for which in range(2):

                    @pl.when(slot == 2 * half + which)
                    def _(other=other, half=half, which=which):
                        rows = slice(8 * half, 8 * half + 8)
                        outs[other][...] = own_zero[rows] if which == 0 else own[rows]


def second_lift_kernel(place, *refs):
    third, low_even, low_odd, halo_a, halo_b = refs[:5]
    weights, outs, (target, high, low, slots, *spares) = refs[5:9], refs[9:13], refs[13:]
    chip, odd_ring = place[0], place[2] % 2 == 1
    target[LAYERS : LAYERS + ROWS] = low_odd[...]
    place_halo(target, halo_a, halo_b, LAYERS, odd_ring)
    lift(third, target, low_even, high, spares, weights, low, edges(place))
    own_low = own_columns(low[...])
    own_high = own_columns(high[LAYERS : LAYERS + ROWS])
    for half in range(2):
        slots[2 * half] = own_low[8 * half : 8 * half + 8]
        slots[2 * half + 1] = own_high[8 * half : 8 * half + 8]
    for other in range(4):
        outs[other][...] = slots[chip ^ other]


def toeplitz_kernel(place, predict_ref, update_ref, *outs):
    del place
    none = jnp.zeros((C, C), BF16)
    for kernels, targets in ((predict_ref, outs[:2]), (update_ref, outs[2:])):
        for level in range(2):
            for layer in range(LAYERS):
                for s in range(3):
                    taps = [kernels[level, layer, r, s] for r in range(3)]
                    for shift in range(2):
                        row = [none] * 4
                        row[shift : shift + 3] = taps
                        start = C * (2 * s + shift)
                        targets[level][layer, start : start + C, :] = jnp.concatenate(row, axis=1)


def spread_bias(biases):
    return jnp.broadcast_to(jnp.tile(biases, (1, 1, 2))[..., None], (2, LAYERS, 2 * C, 128))


def to_core(x):
    return lax.ppermute(x, "frame", [(i, i ^ 1) for i in range(4)])


def to_chip(x, other):
    if other == 0:
        return x
    if other == 1:
        return lax.ppermute(x, "frame", [(i, i ^ 2) for i in range(4)])
    tiles = lax.axis_size("tile")
    if other == 2:
        return lax.ppermute(x, "tile", [(i, i ^ 1) for i in range(tiles)])
    return lax.ppermute(
        x,
        ("frame", "tile"),
        [(f * tiles + t, (f ^ 2) * tiles + (t ^ 1)) for f in range(4) for t in range(tiles)],
    )


def with_rings(first, second):
    tiles = lax.axis_size("tile")
    one = [(t, t ^ 2) for t in range(tiles)]
    two = []
    for t in range(tiles):
        target = t + 2 if (t // 2) % 2 == 1 else t - 2
        if 0 <= target < tiles:
            two.append((t, target))
    return lax.ppermute(first, "tile", one), lax.ppermute(second, "tile", two)


def local(frames, predict_w, predict_b, update_w, update_b):
    position, tile = lax.axis_index("frame"), lax.axis_index("tile")
    core = position % 2
    chip = 2 * (tile % 2) + position // 2
    ring = tile // 2
    place = jnp.stack([chip, core, ring]).astype(jnp.int32)
    odd_ring = ring % 2 == 1
    x = frames[0].reshape(8 * C, 2048)

    pair_flops = 2 * 6 * C * 4 * C * LANES

    def split(which):
        (out,) = call(
            functools.partial(split_kernel, which),
            [field(4, 6, C, LANES)],
            [pltpu.VMEM((3, 8 * C, 128), F32)],
            2 * 4 * 512 * 512 * LANES,
            f"split_{which}",
            place,
            x,
        )
        return out

    def scratch(*rows):
        return [pltpu.VMEM((count, C, LANES), BF16) for count in rows]

    passed = to_core(split(1))
    kept = split(0)
    is_even = core == 0

    def chosen(first, second, other):
        mine = lax.dynamic_index_in_dim(first, chip ^ other, 0, False)
        theirs = lax.dynamic_index_in_dim(second, chip ^ other, 0, False)
        return jnp.where(is_even, mine, theirs)

    even_sent = [chosen(kept, passed, other) for other in range(4)]
    kept, passed, *even_sent = lax.optimization_barrier((kept, passed, *even_sent))
    evens = [to_chip(x, other) for other, x in enumerate(even_sent)]
    odds = [chosen(passed, kept, 0)]
    for other in range(1, 4):
        evens[other], sent = lax.optimization_barrier((evens[other], chosen(passed, kept, other)))
        odds.append(to_chip(sent, other))

    def half(pieces, which):
        late = ((chip // 2) ^ which) == 1
        return [jnp.where(late, pieces[2 + j], pieces[j]) for j in range(2)]

    even_low, even_high = half(evens, 0), half(evens, 1)
    even_halo = with_rings(
        jnp.stack([jnp.where(odd_ring, a, b) for a, b in zip(even_low, even_high)]),
        jnp.stack([jnp.where(odd_ring, b, a) for a, b in zip(even_low, even_high)]),
    )
    odd_low = [x[:3] for x in half(odds, 0)]
    odd_high = [x[3:] for x in half(odds, 1)]
    odd_halo = with_rings(
        jnp.stack([jnp.where(odd_ring, a, b) for a, b in zip(odd_low, odd_high)]),
        jnp.stack([jnp.where(odd_ring, b, a) for a, b in zip(odd_low, odd_high)]),
    )

    pw0, pw1, uw0, uw1 = call(
        toeplitz_kernel,
        [field(LAYERS, 6 * C, 4 * C)] * 4,
        [],
        2 * 4 * 512 * 512 * LANES,
        "toeplitz",
        place,
        predict_w,
        update_w,
    )
    pb, ub = spread_bias(predict_b), spread_bias(update_b)

    (third,) = call(
        first_hidden_kernel,
        [field(2, ROWS + 10, C, LANES)],
        scratch(32, 30, 28),
        84 * pair_flops,
        "first_hidden",
        place,
        *evens,
        *even_halo,
        pw0,
        pb[0],
    )

    whole = field(ROWS, C, LANES)
    owned = field(8, C, OWN)
    low, halo_low, owns = [], [], []
    for pair in range(2):
        depth = 2 * LAYERS if pair == 0 else LAYERS
        strip = field(3 * depth // 4, C, LANES)
        result, strip_a, strip_b, *owns = call(
            functools.partial(first_lift_kernel, pair, depth),
            [whole, strip, strip, *([field(ROWS, C, OWN)] if pair == 0 else [owned] * 4)],
            scratch(24, 16, 24, 22, 20, 18),
            50 * pair_flops,
            f"first_lift_{pair}",
            place,
            third,
            *evens,
            *odds,
            *odd_halo,
            pw0,
            pb[0],
            uw0,
            ub[0],
            *owns,
        )
        low.append(result)
        halo_low.append(with_rings(strip_a, strip_b))

    (third,) = call(
        second_hidden_kernel,
        [field(ROWS + 10, C, LANES)],
        scratch(32, 30, 28),
        42 * pair_flops,
        "second_hidden",
        place,
        low[0],
        *halo_low[0],
        pw1,
        pb[1],
    )
    ones = [to_chip(x, other) for other, x in enumerate(owns)]
    ones_other = [to_core(x) for x in ones]
    owns = call(
        second_lift_kernel,
        [owned] * 4,
        scratch(24, 24, 16) + [pltpu.VMEM((4, 8, C, OWN), BF16)] + scratch(22, 20, 18),
        50 * pair_flops,
        "second_lift",
        place,
        third,
        *low,
        *halo_low[1],
        pw1,
        pb[1],
        uw1,
        ub[1],
    )
    twos = [to_chip(x, other) for other, x in enumerate(owns)]
    twos_other = [to_core(x) for x in twos]
    (out,) = call(
        join_kernel,
        [field(8 * C, 2048)],
        [pltpu.VMEM((2, 8 * C, 128), F32)],
        0,
        "join",
        place,
        *twos,
        *twos_other,
        *ones,
        *ones_other,
    )
    return out.reshape(1, C, 8, 2048)


def solution(mesh):
    in_specs = (P("frame", None, "tile", None), P(), P(), P(), P())
    out_specs = P("frame", None, "tile", None)
    return jax.shard_map(local, mesh=mesh, in_specs=in_specs, out_specs=out_specs, check_vma=False)
```

```python
import functools

import jax
import jax.numpy as jnp
from jax import lax
from jax.experimental import pallas as pl
from jax.experimental.pallas import tpu as pltpu
from jax.sharding import PartitionSpec as P

LAYERS = 4
C = 64
ROWS = 16
LANES = 384
OWN = 256
EDGE = 64
BF16 = jnp.bfloat16
F32 = jnp.float32
VMEM_LIMIT = 24 * 1024 * 1024
GROUP = 4


def call(kernel, out_shapes, scratch, flops, name, *args):
    nbytes = sum(a.size * a.dtype.itemsize for a in args) + sum(
        s.size * s.dtype.itemsize for s in out_shapes
    )
    return pl.pallas_call(
        kernel,
        out_shape=out_shapes,
        in_specs=[pl.BlockSpec(memory_space=pltpu.SMEM)]
        + [pl.BlockSpec(memory_space=pltpu.VMEM)] * (len(args) - 1),
        out_specs=[pl.BlockSpec(memory_space=pltpu.VMEM)] * len(out_shapes),
        scratch_shapes=scratch,
        compiler_params=pltpu.CompilerParams(vmem_limit_bytes=VMEM_LIMIT),
        cost_estimate=pl.CostEstimate(flops=flops, bytes_accessed=nbytes, transcendentals=0),
        name=name,
    )(*args)


def field(*dims):
    return jax.ShapeDtypeStruct(dims, BF16)


def rolled(value, amount):
    return jnp.concatenate(
        [pltpu.roll(value[:, 128 * v : 128 * (v + 1)], amount % 128, 1) for v in range(3)], axis=1
    )


def lane_in_block():
    return lax.broadcasted_iota(jnp.int32, (C, LANES), 1) % 128


def packed(rows):
    lane = lane_in_block()
    free = (lane < 16) | (lane >= 112)
    return [jnp.where(free, rolled(rows[3], 96 - 32 * j), rows[j]) for j in range(3)]


def unpacked(rows):
    lane = lane_in_block()
    parts = [rolled(rows[j], 32 * j - 96) for j in range(3)]
    fourth = jnp.where(lane < 48, parts[0], jnp.where(lane < 80, parts[1], parts[2]))
    return [*rows, fourth]


def unpack_into(field_ref, start, source, count):
    for group in range(count // 4):
        rows = unpacked([source[3 * group + j] for j in range(3)])
        for j in range(4):
            field_ref[start + 4 * group + j] = rows[j]


def split_kernel(which, place, x_ref, out_ref, spread):
    core = place[1]
    source = lax.broadcasted_iota(jnp.int32, (512, LANES), 0)
    column = lax.broadcasted_iota(jnp.int32, (512, LANES), 1)
    pick = jnp.where(source == 3 * (column % 128) + column // 128 + 128 - EDGE, 1.0, 0.0)
    pick = pick.astype(BF16)

    def windows(group):
        for slot in range(4):
            start = 256 * (4 * group + slot) - 128
            low, high = max(start, 0), min(start + 512, 2048)
            window = jnp.dot(
                x_ref[:, low:high], pick[low - start : high - start], preferred_element_type=F32
            )
            for v in range(3):
                spread[v] = window[:, 128 * v : 128 * (v + 1)]
            for half in range(2):
                rows = packed(
                    [
                        jnp.concatenate(
                            [spread[v, pl.ds(row, C, stride=8), :] for v in range(3)], axis=1
                        ).astype(BF16)
                        for row in range(4 * half, 4 * half + 4)
                    ]
                )
                for j in range(3):
                    out_ref[slot, 3 * half + j] = rows[j]

    for group in range(2):
        pl.when((core ^ which) == group)(functools.partial(windows, group))


def own_columns(value):
    source = lax.broadcasted_iota(jnp.int32, (LANES, OWN), 0)
    column = lax.broadcasted_iota(jnp.int32, (LANES, OWN), 1)
    pick = jnp.where(3 * (source % 128) + source // 128 == column + EDGE, 1.0, 0.0).astype(BF16)
    rows = value.shape[0]
    flat = jnp.dot(value.reshape(rows * C, LANES), pick, preferred_element_type=F32)
    return flat.astype(BF16).reshape(rows, C, OWN)


def join_kernel(others, place, *refs):
    count = 2 * len(others)
    pieces, (out_ref, spread, staged, sems) = refs[: 2 * count], refs[-4:]
    chip, core = place[0], place[1]

    def joined(group):
        copies = []
        for index in range(count):
            side, other = index // len(others), others[index % len(others)]
            piece = pieces[count * group + index]
            for row in range(8):
                values = piece[row].astype(F32)
                for v in range(2):
                    spread[v, pl.ds(row, C, stride=8), :] = values[:, 128 * v : 128 * (v + 1)]
            for v in range(2):
                staged[index, :, 128 * v : 128 * (v + 1)] = spread[v].astype(BF16)
            column = pl.multiple_of((4 * (group ^ side) + (chip ^ other)) * OWN, OWN)
            copies.append(
                pltpu.make_async_copy(
                    staged.at[index], out_ref.at[:, pl.ds(column, OWN)], sems.at[index]
                )
            )
            copies[-1].start()
        for copy in copies:
            copy.wait()

    for group in range(2):
        pl.when(core == group)(functools.partial(joined, group))


def join(others, place, pieces, base=None):
    count = 2 * len(others)
    args = [place, *pieces] + ([] if base is None else [base])
    return pl.pallas_call(
        functools.partial(join_kernel, others),
        out_shape=field(8 * C, 2048),
        in_specs=[pl.BlockSpec(memory_space=pltpu.SMEM)]
        + [pl.BlockSpec(memory_space=pltpu.VMEM)] * len(pieces)
        + [pl.BlockSpec(memory_space=pl.ANY)] * (base is not None),
        out_specs=pl.BlockSpec(memory_space=pl.ANY),
        scratch_shapes=[
            pltpu.VMEM((2, 8 * C, 128), F32),
            pltpu.VMEM((count, 8 * C, OWN), BF16),
            pltpu.SemaphoreType.DMA((count,)),
        ],
        input_output_aliases={} if base is None else {len(args) - 1: 0},
        compiler_params=pltpu.CompilerParams(vmem_limit_bytes=VMEM_LIMIT),
        cost_estimate=pl.CostEstimate(
            flops=0, bytes_accessed=count * 4 * 8 * C * OWN, transcendentals=0
        ),
        name=f"join_{len(others)}",
    )(*args)


def edges(place):
    lane = lax.broadcasted_iota(jnp.int32, (1, 128), 1)
    window = 4 * place[1] + place[0]
    left = jnp.where((lane == 21) & (window == 0), 0.0, 1.0)
    right = jnp.where((lane == 106) & (window == 7), 0.0, 1.0)
    top = jnp.where(place[2] == 0, 0.0, 1.0)
    bottom = jnp.where(place[2] == 15, 0.0, 1.0)
    return left, right, top, bottom


def conv(source, count, weights, bias, left, right, store):
    for first in range(0, count // 2, GROUP):
        pairs = range(first, min(first + GROUP, count // 2))
        stack = jnp.concatenate(
            [source[2 * j : 2 * j + 4].reshape(4 * C, LANES) for j in pairs], axis=1
        )
        product = jnp.dot(weights, stack, preferred_element_type=F32)
        for place, j in enumerate(pairs):
            part = [
                [
                    product[
                        2 * C * s : 2 * C * (s + 1),
                        LANES * place + 128 * v : LANES * place + 128 * (v + 1),
                    ]
                    for v in range(3)
                ]
                for s in range(3)
            ]
            blocks = [
                pltpu.roll(part[0][2], 1, 1) + part[1][0] + part[2][1] + bias,
                part[0][0] * left + part[1][1] + part[2][2] * right + bias,
                part[0][1] + part[1][2] + pltpu.roll(part[2][0], 127, 1) + bias,
            ]
            total = jnp.concatenate(blocks, axis=1)
            store(2 * j, total[:C])
            store(2 * j + 1, total[C:])


def hidden_layers(source, targets, halo, weights, biases, edge):
    left, right, top, bottom = edge
    for layer, target in enumerate(targets):
        halo -= 1
        count = source.shape[0] - 2

        def keep(row, value, halo=halo, target=target):
            value = jnp.maximum(value, 0.0)
            if row == halo - 1:
                value = value * top
            if row == halo + ROWS:
                value = value * bottom
            target[row] = value.astype(BF16)

        conv(source, count, weights[layer], biases[layer], left, right, keep)
        source = target
    return source


def lift(third, target, base, high, spares, weights, low, edge):
    predict_w, predict_b, update_w, update_b = weights
    left, right, top, bottom = edge

    def finish_high(row, value):
        value = target[row].astype(F32) - value
        if row == LAYERS - 1:
            value = value * top
        if row == LAYERS + ROWS:
            value = value * bottom
        high[row] = value.astype(BF16)

    conv(third, ROWS + 8, predict_w[3], predict_b[3], left, right, finish_high)

    def finish_low(row, value):
        low[row] = (base[row].astype(F32) + value).astype(BF16)

    source = hidden_layers(high, spares, LAYERS, update_w, update_b, edge)
    conv(source, ROWS, update_w[3], update_b[3], left, right, finish_low)


def place_halo(field_ref, first, second, depth, ring_is_odd):
    low, high = 0, depth + ROWS
    unpack_into(field_ref, jnp.where(ring_is_odd, low, high), first, depth)
    unpack_into(field_ref, jnp.where(ring_is_odd, high, low), second, depth)


def clear_outside(field_ref, halo, place):
    for ring, row in ((0, halo - 1), (15, halo + ROWS)):

        @pl.when(place[2] == ring)
        def _(row=row):
            field_ref[row] = jnp.zeros((C, LANES), BF16)


def place_pieces(field_ref, pieces, pair, chip, offset):
    for other in range(4):
        slot = chip ^ other

        @pl.when((slot & 1) == pair)
        def _(other=other, slot=slot):
            unpack_into(field_ref, offset + 8 * (slot // 2), pieces[other], 8)


def strips(result, first_ref, second_ref, depth, ring_is_odd):
    for ref, start in (
        (first_ref, jnp.where(ring_is_odd, 0, ROWS - depth)),
        (second_ref, jnp.where(ring_is_odd, ROWS - depth, 0)),
    ):
        for group in range(depth // 4):
            rows = packed([result[start + 4 * group + j] for j in range(4)])
            for j in range(3):
                ref[3 * group + j] = rows[j]


def first_hidden_kernel(place, *refs):
    evens, halo_a, halo_b, weights, biases, out, source, spare_a, spare_b = (refs[:4], *refs[4:])
    chip, odd_ring = place[0], place[2] % 2 == 1
    for pair in range(2):
        entry = (chip & 1) ^ pair
        place_pieces(source, evens, pair, chip, 2 * LAYERS)
        place_halo(source, halo_a.at[entry], halo_b.at[entry], 2 * LAYERS, odd_ring)
        clear_outside(source, 2 * LAYERS, place)
        targets = (spare_a, spare_b, out.at[pair])
        hidden_layers(source, targets, 2 * LAYERS, weights, biases, edges(place))


def second_hidden_kernel(place, *refs):
    low_even, halo_a, halo_b, weights, biases, out, source, spare_a, spare_b = refs
    odd_ring = place[2] % 2 == 1
    source[2 * LAYERS : 2 * LAYERS + ROWS] = low_even[...]
    place_halo(source, halo_a, halo_b, 2 * LAYERS, odd_ring)
    clear_outside(source, 2 * LAYERS, place)
    targets = (spare_a, spare_b, out)
    hidden_layers(source, targets, 2 * LAYERS, weights, biases, edges(place))


def first_lift_kernel(pair, depth, place, *refs):
    third, evens, odds, halo_a, halo_b = refs[0], refs[1:5], refs[5:9], refs[9], refs[10]
    weights, refs = refs[11:15], refs[15:]
    if pair == 1:
        own_zero, refs = refs[0], refs[1:]
    low, strip_a, strip_b = refs[:3]
    outs, (target, base, high, *spares) = refs[3:-6], refs[-6:]
    chip, odd_ring = place[0], place[2] % 2 == 1
    entry = (chip & 1) ^ pair
    place_pieces(target, odds, pair, chip, LAYERS)
    place_halo(target, halo_a.at[entry], halo_b.at[entry], LAYERS, odd_ring)
    place_pieces(base, evens, pair, chip, 0)
    lift(third.at[pair], target, base, high, spares, weights, low, edges(place))
    strips(low, strip_a, strip_b, depth, odd_ring)
    own = own_columns(high[LAYERS : LAYERS + ROWS])
    if pair == 0:
        outs[0][...] = own
    else:
        for other in range(4):
            slot = chip ^ other
            for half in range(2):
                for which in range(2):

                    @pl.when(slot == 2 * half + which)
                    def _(other=other, half=half, which=which):
                        rows = slice(8 * half, 8 * half + 8)
                        outs[other][...] = own_zero[rows] if which == 0 else own[rows]


def second_lift_kernel(place, *refs):
    third, low_even, low_odd, halo_a, halo_b = refs[:5]
    weights, outs, (target, high, low, slots, *spares) = refs[5:9], refs[9:13], refs[13:]
    chip, odd_ring = place[0], place[2] % 2 == 1
    target[LAYERS : LAYERS + ROWS] = low_odd[...]
    place_halo(target, halo_a, halo_b, LAYERS, odd_ring)
    lift(third, target, low_even, high, spares, weights, low, edges(place))
    own_low = own_columns(low[...])
    own_high = own_columns(high[LAYERS : LAYERS + ROWS])
    for half in range(2):
        slots[2 * half] = own_low[8 * half : 8 * half + 8]
        slots[2 * half + 1] = own_high[8 * half : 8 * half + 8]
    for other in range(4):
        outs[other][...] = slots[chip ^ other]


def toeplitz_kernel(place, predict_ref, update_ref, *outs):
    del place
    none = jnp.zeros((C, C), BF16)
    for kernels, targets in ((predict_ref, outs[:2]), (update_ref, outs[2:])):
        for level in range(2):
            for layer in range(LAYERS):
                for s in range(3):
                    taps = [kernels[level, layer, r, s] for r in range(3)]
                    for shift in range(2):
                        row = [none] * 4
                        row[shift : shift + 3] = taps
                        start = C * (2 * s + shift)
                        targets[level][layer, start : start + C, :] = jnp.concatenate(row, axis=1)


def spread_bias(biases):
    return jnp.broadcast_to(jnp.tile(biases, (1, 1, 2))[..., None], (2, LAYERS, 2 * C, 128))


def to_core(x):
    return lax.ppermute(x, "frame", [(i, i ^ 1) for i in range(4)])


def to_chip(x, other):
    if other == 0:
        return x
    if other == 1:
        return lax.ppermute(x, "frame", [(i, i ^ 2) for i in range(4)])
    tiles = lax.axis_size("tile")
    if other == 2:
        return lax.ppermute(x, "tile", [(i, i ^ 1) for i in range(tiles)])
    return lax.ppermute(
        x,
        ("frame", "tile"),
        [(f * tiles + t, (f ^ 2) * tiles + (t ^ 1)) for f in range(4) for t in range(tiles)],
    )


def with_rings(first, second):
    tiles = lax.axis_size("tile")
    two = []
    for f in range(4):
        for t in range(tiles):
            target = t + 2 if (t // 2) % 2 == 1 else t - 2
            inside = 0 <= target < tiles
            two.append((f * tiles + t, f * tiles + target if inside else (f ^ 1) * tiles + t))
    return (
        lax.ppermute(first, "tile", [(t, t ^ 2) for t in range(tiles)]),
        lax.ppermute(second, ("frame", "tile"), two),
    )


def local(frames, predict_w, predict_b, update_w, update_b):
    position, tile = lax.axis_index("frame"), lax.axis_index("tile")
    core = position % 2
    chip = 2 * (tile % 2) + position // 2
    ring = tile // 2
    place = jnp.stack([chip, core, ring]).astype(jnp.int32)
    odd_ring = ring % 2 == 1
    x = frames[0].reshape(8 * C, 2048)

    pair_flops = 2 * 6 * C * 4 * C * LANES

    def split(which):
        (out,) = call(
            functools.partial(split_kernel, which),
            [field(4, 6, C, LANES)],
            [pltpu.VMEM((3, 8 * C, 128), F32)],
            2 * 4 * 512 * 512 * LANES,
            f"split_{which}",
            place,
            x,
        )
        return out

    def scratch(*rows):
        return [pltpu.VMEM((count, C, LANES), BF16) for count in rows]

    passed = to_core(split(1))
    kept = split(0)
    is_even = core == 0

    def chosen(first, second, other):
        mine = lax.dynamic_index_in_dim(first, chip ^ other, 0, False)
        theirs = lax.dynamic_index_in_dim(second, chip ^ other, 0, False)
        return jnp.where(is_even, mine, theirs)

    even_sent = [chosen(kept, passed, other) for other in range(4)]
    kept, passed, *even_sent = lax.optimization_barrier((kept, passed, *even_sent))
    evens = [to_chip(x, other) for other, x in enumerate(even_sent)]
    odds = [chosen(passed, kept, 0)]
    for other in range(1, 4):
        evens[other], sent = lax.optimization_barrier((evens[other], chosen(passed, kept, other)))
        odds.append(to_chip(sent, other))

    def half(pieces, which):
        late = ((chip // 2) ^ which) == 1
        return [jnp.where(late, pieces[2 + j], pieces[j]) for j in range(2)]

    even_low, even_high = half(evens, 0), half(evens, 1)
    even_halo = with_rings(
        jnp.stack([jnp.where(odd_ring, a, b) for a, b in zip(even_low, even_high)]),
        jnp.stack([jnp.where(odd_ring, b, a) for a, b in zip(even_low, even_high)]),
    )
    odd_low = [x[:3] for x in half(odds, 0)]
    odd_high = [x[3:] for x in half(odds, 1)]
    odd_halo = with_rings(
        jnp.stack([jnp.where(odd_ring, a, b) for a, b in zip(odd_low, odd_high)]),
        jnp.stack([jnp.where(odd_ring, b, a) for a, b in zip(odd_low, odd_high)]),
    )

    pw0, pw1, uw0, uw1 = call(
        toeplitz_kernel,
        [field(LAYERS, 6 * C, 4 * C)] * 4,
        [],
        2 * 4 * 512 * 512 * LANES,
        "toeplitz",
        place,
        predict_w,
        update_w,
    )
    pb, ub = spread_bias(predict_b), spread_bias(update_b)

    (third,) = call(
        first_hidden_kernel,
        [field(2, ROWS + 10, C, LANES)],
        scratch(32, 30, 28),
        84 * pair_flops,
        "first_hidden",
        place,
        *evens,
        *even_halo,
        pw0,
        pb[0],
    )

    whole = field(ROWS, C, LANES)
    owned = field(8, C, OWN)
    low, halo_low, owns = [], [], []
    for pair in range(2):
        depth = 2 * LAYERS if pair == 0 else LAYERS
        strip = field(3 * depth // 4, C, LANES)
        result, strip_a, strip_b, *owns = call(
            functools.partial(first_lift_kernel, pair, depth),
            [whole, strip, strip, *([field(ROWS, C, OWN)] if pair == 0 else [owned] * 4)],
            scratch(24, 16, 24, 22, 20, 18),
            50 * pair_flops,
            f"first_lift_{pair}",
            place,
            third,
            *evens,
            *odds,
            *odd_halo,
            pw0,
            pb[0],
            uw0,
            ub[0],
            *owns,
        )
        low.append(result)
        halo_low.append(with_rings(strip_a, strip_b))

    (third,) = call(
        second_hidden_kernel,
        [field(ROWS + 10, C, LANES)],
        scratch(32, 30, 28),
        42 * pair_flops,
        "second_hidden",
        place,
        low[0],
        *halo_low[0],
        pw1,
        pb[1],
    )
    ones = [to_chip(x, other) for other, x in enumerate(owns)]
    ones_other = [to_core(x) for x in ones]
    owns = call(
        second_lift_kernel,
        [owned] * 4,
        scratch(24, 24, 16) + [pltpu.VMEM((4, 8, C, OWN), BF16)] + scratch(22, 20, 18),
        50 * pair_flops,
        "second_lift",
        place,
        third,
        *low,
        *halo_low[1],
        pw1,
        pb[1],
        uw1,
        ub[1],
    )
    twos = [to_chip(x, other) for other, x in enumerate(owns)]
    twos_other = [to_core(x) for x in twos]
    columns = (twos, twos_other, ones, ones_other)
    out = join((0, 1, 3), place, [x[other] for x in columns for other in (0, 1, 3)])
    out = join((2,), place, [x[2] for x in columns], out)
    return out.reshape(1, C, 8, 2048)


def solution(mesh):
    in_specs = (P("frame", None, "tile", None), P(), P(), P(), P())
    out_specs = P("frame", None, "tile", None)
    return jax.shard_map(local, mesh=mesh, in_specs=in_specs, out_specs=out_specs, check_vma=False)
```
